32 devices in a mesh: tile: 32 (over z, y, x, core), fit: 1.
Axes of the slice: x: 2, y: 2, z: 4, core: 2. Of those that a mesh axis runs over, the one named last changes fastest.
Arguments:
- factors: bfloat16 [32, 128, 128, 128], P('tile', 'fit'), may hold values from -0.21875 to 0.21875
- amplitudes: bfloat16 [64, 128, 128], P('tile'), may hold values from -6 to 6
- left_step: int32 [64, 13], P('tile'), may hold values from -1 to 1
- right_step: int32 [64, 13], P('tile'), may hold values from -1 to 1
- amp_owner: int32 [64, 13], P('tile'), may hold values from 0 to 31, all different within a row; in each aligned block of 2 rows (0 to 1, 2 to 3, ...) no two rows name the same one
- amp_slot: int32 [64, 13], P('tile'), may hold values from 0 to 1
Outputs:
- residual: bfloat16 [64, 128, 128], P('tile', 'fit')
The draws below stay inside these ranges and needn't reach their ends.
Inputs may be any that keep to these rules, and one draw needn't show every extreme that they name: `amp_owner`: among the 13 terms of the 2 residual tiles of one device, no owner index is named more than 1 times, a bound that some block reaches.
All inputs are finite; a program needn't handle non-finite values.
Results may differ from the reference program's by a relative error of at most 0.0049.
Values may be sent and summed in bfloat16 or wider, within the bound.
No kernel may reach another device: no remote copies, remote signals or barrier semaphores. Data moves between devices by JAX's collectives and lax.ppermute only.
A program may use at most 64 MiB of HBM per device.

```python
import math
import jax
import jax.numpy as jnp
import numpy as np
from jax import lax

W = 128
NAUX = 128
NZ_DEV = 2
TERMS = 13
NF = 32
NNZ = 64
CAP = 1
N_TILE = 32


def plant(drawn, own_key, smallest, high):
    place = [jax.random.randint(jax.random.fold_in(own_key, axis), (), 0, length) for axis, length in enumerate(drawn.shape)]
    main_axis = drawn.shape.index(max(drawn.shape))
    next_to = place[:main_axis] + [(place[main_axis] + 1) % drawn.shape[main_axis]] + place[main_axis + 1:]
    return drawn.at[tuple(place)].set(smallest).at[tuple(next_to)].set(high)


def shard_levels(stream_key, extent, pieces, smallest, high):
    loudness = 1.0
    for dim, shards_of in pieces:
        draws = jax.random.uniform(jax.random.fold_in(jax.random.fold_in(stream_key, 6), dim), (shards_of,), jnp.float32, smallest / len(pieces), high / len(pieces))
        loudness = loudness * jnp.repeat(jnp.exp(draws), extent[dim] // shards_of).reshape((-1,) + (1,) * (len(extent) - 1 - dim))
    return loudness


def shared_out(stream_key, own, number, rows, amount, top, limit, lean):
    ranking = jax.random.permutation(stream_key, amount)
    heavy_load, ordinary = load_shares(amount, rows * top, limit, lean, True), load_shares(amount, rows * top, limit, lean, False)
    places = jnp.arange(amount)

    def named(lengths, rotation):
        used = int((lengths > 0).sum())
        fixed = max(1, used // 4)
        passed = fixed + (places - fixed + rotation * (used - fixed)) % max(1, amount - fixed)
        return jnp.zeros((amount,), jnp.int32).at[ranking[jnp.where(places < fixed, places, passed)]].set(jnp.asarray(lengths, jnp.int32))

    lengths = jnp.where(number % 4 == 0, named(heavy_load, number // 4), named(ordinary, number - number // 4 - 1))
    mixed = jax.random.permutation(jax.random.fold_in(own, 3), amount)
    source_of, receiver = mixed[0:amount // 2 * 2:2], mixed[1:amount // 2 * 2:2]
    room = jnp.minimum(lengths[source_of] - 1, limit - lengths[receiver]) // 2
    room = jnp.where((source_of == ranking[0]) | (receiver == ranking[0]) | (lengths[receiver] == 0), 0, jnp.maximum(room, 0))
    passed = jax.random.randint(jax.random.fold_in(own, 4), (amount // 2,), 0, 1 << 20) % (room + 1)
    lengths = lengths.at[source_of].add(-passed).at[receiver].add(passed)
    members = jnp.searchsorted(jnp.cumsum(lengths), jnp.arange(rows * top), side="right").astype(jnp.int32)
    listing = members.reshape(top, rows).T
    listing = listing[jax.random.permutation(jax.random.fold_in(own, 1), rows)]
    rotation = jax.random.randint(jax.random.fold_in(own, 2), (rows, 1), 0, top)
    return jnp.take_along_axis(listing, (jnp.arange(top)[None, :] + rotation) % top, axis=1)


def load_shares(count, total, limit, slope, full):
    loads = [(1 << 20) // math.isqrt(grade ** slope) + 1 for grade in range(1, count + 1)]
    largest = limit if full else min(limit, max(-(-total // count), total * loads[0] // sum(loads)))
    least = 1 if total - largest >= count - 1 else 0
    given, spare = [largest] + [least] * (count - 1), total - largest - least * (count - 1)
    while spare > 0:
        movable = [i for i in range(1, count) if given[i] < largest] or [i for i in range(1, count) if given[i] < limit]
        mass, budget = sum([loads[i] for i in movable]), spare
        for i in movable:
            extra = min(limit - given[i], max(1, budget * loads[i] // mass), spare)
            given[i] = given[i] + extra
            spare = spare - extra
    return np.array(given)


def centred(key, extent, spread, bound, pieces=(), dtype=jnp.bfloat16):
    array = spread * jax.random.normal(key, extent, jnp.float32)
    if pieces:
        array = array * shard_levels(key, extent, pieces, -0.22, 0.18)
    return jnp.clip(array, -bound, bound).astype(dtype)


def setup_inputs(seed: int = 0) -> dict:
    keys = jax.random.split(jax.random.key(seed), 7)
    factors = centred(keys[0], (NF, NAUX, W, W), ((W * W * NAUX * TERMS) ** -0.25), 0.21875, ((0, 32),))
    amplitudes = centred(keys[1], (NNZ, W, W), 1.0, 6.0, ((0, 32),))
    left_step = plant(jax.random.randint(keys[2], (NNZ, TERMS), -1, 2), jax.random.fold_in(keys[2], 1), -1, 1).astype(jnp.int32)
    right_step = plant(jax.random.randint(keys[3], (NNZ, TERMS), -1, 2), jax.random.fold_in(keys[3], 1), -1, 1).astype(jnp.int32)
    amp_owner_keys = jax.random.split(jax.random.fold_in(keys[4], 1), NNZ // NZ_DEV)
    amp_owner_turns = jax.random.permutation(jax.random.fold_in(keys[4], 3), NNZ // NZ_DEV)
    amp_owner = jax.vmap(lambda own, number: shared_out(jax.random.fold_in(keys[4], 2), own, number, NZ_DEV, N_TILE, TERMS, CAP, 2))(amp_owner_keys, amp_owner_turns).reshape((NNZ, TERMS))
    amp_slot = plant(jax.random.randint(keys[5], (NNZ, TERMS), 0, NZ_DEV), jax.random.fold_in(keys[5], 1), 0, NZ_DEV - 1).astype(jnp.int32)
    return {"factors": factors, "amplitudes": amplitudes, "left_step": left_step, "right_step": right_step, "amp_owner": amp_owner, "amp_slot": amp_slot}


def reference(factors, amplitudes, left_step, right_step, amp_owner, amp_slot):
    owner_row = (jnp.arange(NNZ) // NZ_DEV).astype(jnp.int32)[:, None]
    left_tile = jnp.clip(owner_row + left_step, 0, NF - 1).astype(jnp.int32)
    right_tile = jnp.clip(owner_row + right_step, 0, NF - 1).astype(jnp.int32)
    source = (amp_owner * NZ_DEV + amp_slot).astype(jnp.int32)

    def one_tile(ids):
        left_row, right_row, source_row = ids

        def add_term(total, item):
            left_id, right_id, source_id = item
            right_fac = factors[right_id].astype(jnp.float32)
            left_fac = factors[left_id].astype(jnp.float32)
            ampl = amplitudes[source_id].astype(jnp.float32)
            half = jnp.einsum("cd,pbd->pcb", ampl, right_fac).astype(jnp.bfloat16)
            term = jnp.einsum("pac,pcb->ab", left_fac, half.astype(jnp.float32))
            return total + term, None

        total, _ = lax.scan(add_term, jnp.zeros((W, W), jnp.float32), (left_row, right_row, source_row))
        return total.astype(jnp.bfloat16)

    return lax.map(one_tile, (left_tile, right_tile, source))
```

```python
import functools

import jax
import jax.numpy as jnp
from jax import lax
from jax.experimental import pallas as pl
from jax.experimental.pallas import tpu as pltpu
from jax.sharding import PartitionSpec as P

GROUP = 8
QUADS = 4
PIECES = 2
ORDER = (0, 3, 1, 2)
ROWS = 16
DEPTH = 16
LIMIT = 32 * 1024 * 1024
SMALL = 6 * 1024 * 1024
VMEM = pl.BlockSpec(memory_space=pltpu.VMEM)
SMEM = pl.BlockSpec(memory_space=pltpu.SMEM)
NT = (((1,), (1,)), ((), ()))
FREE = pl.CostEstimate(flops=0, bytes_accessed=0, transcendentals=0)


def pack_kernel(tiles, *refs):
    *sources, out, rows, amps, left, right, owner, slot, sems = refs
    here = lax.axis_index("tile")
    copies = [
        pltpu.make_async_copy(source, held, sems.at[i])
        for i, (source, held) in enumerate(zip(sources, (amps, left, right, owner, slot)))
    ]
    for copy in copies:
        copy.start()
    nz, w, _ = amps.shape
    terms = owner.shape[1]
    rows[...] = jnp.zeros_like(rows)
    for copy in copies:
        copy.wait()
    left_at = jnp.clip(here + left[...], 0, tiles - 1) - here + 1
    right_at = jnp.clip(here + right[...], 0, tiles - 1) - here + 1
    first = lax.broadcasted_iota(jnp.int32, (nz, terms), 0) * 9
    place = first + left_at * 3 + right_at
    turned = first + jnp.where(left_at == 0, 2, left_at - 1) * 3
    turned = turned + jnp.where(right_at == 0, 2, right_at - 1)
    for i, value in enumerate((owner[...], slot[...], place, turned)):
        rows[i * nz:(i + 1) * nz, 0:terms] = value.astype(jnp.float32)
    for s in range(nz):
        out[0, s * w:(s + 1) * w] = amps[s]
    out[0, nz * w:] = rows[...].astype(out.dtype)


def pack(tiles, *sources):
    nz, w, _ = sources[0].shape
    return pl.pallas_call(
        functools.partial(pack_kernel, tiles),
        out_shape=jax.ShapeDtypeStruct((1, nz * w + ROWS, w), sources[0].dtype),
        in_specs=[pl.BlockSpec(memory_space=pl.ANY)] * len(sources),
        out_specs=VMEM,
        scratch_shapes=[pltpu.VMEM((ROWS, w), jnp.float32)]
        + [pltpu.VMEM(source.shape, source.dtype) for source in sources]
        + [pltpu.SemaphoreType.DMA((len(sources),))],
        compiler_params=pltpu.CompilerParams(vmem_limit_bytes=60 * 1024 * 1024),
        cost_estimate=FREE,
        name="pack",
    )(*sources)


def mix_kernel(terms, layers, where, lists_mine, lists_other, amps, *refs):
    *before, out, acc, rows, lists, sem = refs
    column = 1 if before else 0
    w = amps.shape[2]
    nz = acc.shape[0] // 9
    lines = rows.shape[0] // GROUP
    layer, local, core = where[0], where[1], where[3]

    for n, source in enumerate((lists_mine, lists_other)):
        for i in range(QUADS):
            listed = source[i, nz * w:nz * w + ROWS, :].astype(jnp.float32)
            at = (n * QUADS + i) * lines
            rows[at:at + lines] = listed[:lines].astype(jnp.int32)
    copy = pltpu.make_async_copy(rows, lists, sem)
    copy.start()
    copy.wait()

    for step in range(QUADS):
        total = acc if before else out.at[step]
        total[...] = before[0][step] if before else jnp.zeros_like(acc)
        entry = (core * QUADS + step) ^ local
        row = ((entry & 1) * QUADS + (entry >> 1)) * lines

        def add(i, carry):
            for s in range(nz):
                owner = lists[row + s, i]
                slot = lists[row + nz + s, i]
                place = lists[row + (3 if step == 0 else 2) * nz + s, i]
                away = (owner & (GROUP - 1)) ^ local
                turn = layer - (owner >> 3) + layers
                if layers & (layers - 1) == 0:
                    turn = turn & (layers - 1)
                else:
                    turn = lax.rem(turn, layers)
                part = pl.ds(pl.multiple_of(slot * w, w), w)

                @pl.when((away & 1) == column)
                def _():
                    tile = amps[turn * QUADS + (away >> 1), part, :]
                    total[place] = total[place] + tile.astype(jnp.float32)

            return carry

        lax.fori_loop(0, terms, add, 0)
        if not before:
            continue
        for s in range(nz):
            for l in range(3):
                for r in range(3):
                    out[step, (s * 3 + l) * w:(s * 3 + l + 1) * w, r * w:(r + 1) * w] = acc[
                        (s * 3 + l) * 3 + r
                    ].astype(out.dtype)


def mix(where, mine, other, amps, nz, terms, layers, before=()):
    w = amps.shape[2]
    lines = -(-4 * nz // 8) * 8
    first = jax.ShapeDtypeStruct((QUADS, 9 * nz, w, w), jnp.float32)
    second = jax.ShapeDtypeStruct((QUADS, 3 * w * nz, 3 * w), amps.dtype)
    return pl.pallas_call(
        functools.partial(mix_kernel, terms, layers),
        out_shape=second if before else first,
        in_specs=[SMEM] + [VMEM] * (3 + len(before)),
        out_specs=VMEM,
        scratch_shapes=[
            pltpu.VMEM((9 * nz, w, w), jnp.float32),
            pltpu.VMEM((GROUP * lines, w), jnp.int32),
            pltpu.SMEM((GROUP * lines, w), jnp.int32),
            pltpu.SemaphoreType.DMA,
        ],
        compiler_params=pltpu.CompilerParams(vmem_limit_bytes=SMALL),
        cost_estimate=FREE,
        name="mix",
    )(where, mine, other, amps, *before)


def join_kernel(*refs):
    *pieces, out = refs
    size = pieces[0].shape[0]
    for i, piece in enumerate(pieces):
        out[i * size:(i + 1) * size] = piece[...]


def join(pieces):
    size, *rest = pieces[0].shape
    return pl.pallas_call(
        join_kernel,
        out_shape=jax.ShapeDtypeStruct((len(pieces) * size, *rest), pieces[0].dtype),
        in_specs=[VMEM] * len(pieces),
        out_specs=VMEM,
        cost_estimate=FREE,
        compiler_params=pltpu.CompilerParams(vmem_limit_bytes=SMALL),
        name="join",
    )(*pieces)


def sort_kernel(where, a, b, c, d, own_a, own_d, held, mid, halo):
    quad, core = where[2], where[3]
    for t, (tile, own) in enumerate(((a, own_a), (b, None), (c, None), (d, own_d))):
        at = quad ^ t

        def lay(tile, use):
            for_mid = (at == 0) == (core == 1)

            @pl.when(use)
            def _():
                held[at] = tile[...]

            rim = ((at == 0) | (at == QUADS - 1)) & use

            @pl.when(rim & for_mid)
            def _():
                mid[...] = tile[...]

            @pl.when(rim & jnp.logical_not(for_mid))
            def _():
                halo[...] = tile[...]

        if own is None:
            lay(tile, at >= 0)
        else:
            stays = core * QUADS + at == where[1]
            lay(own, stays)
            lay(tile, jnp.logical_not(stays))


def sort(where, tiles, own):
    kind = jax.ShapeDtypeStruct(tiles[0].shape, tiles[0].dtype)
    return pl.pallas_call(
        sort_kernel,
        out_shape=(jax.ShapeDtypeStruct((QUADS,) + kind.shape, kind.dtype), kind, kind),
        in_specs=[SMEM] + [VMEM] * (QUADS + 2),
        out_specs=(VMEM, VMEM, VMEM),
        compiler_params=pltpu.CompilerParams(vmem_limit_bytes=SMALL),
        cost_estimate=FREE,
        name="sort",
    )(where, *tiles, own[0], own[QUADS - 1])


def products(tiles, weights, acc, nz):
    count, w = tiles[0][0].shape[-3:-1]
    depth = next(d for d in (DEPTH, 8, 4, 2, 1) if count % d == 0)
    pair = 2 if depth % 2 == 0 else 1

    def part(step):
        rows = slice(step * depth, (step + 1) * depth)
        x = jnp.concatenate(
            [ref[lead + (rows,)].reshape(depth * w, w) for ref, lead in tiles], axis=1
        )
        half = lax.dot_general(weights, x, NT, preferred_element_type=jnp.float32)
        half = half.astype(x.dtype)
        total = jnp.zeros((w, nz * w), jnp.float32)
        for p in range(0, depth, pair):
            parts = [slice((p + i) * w, (p + i + 1) * w) for i in range(pair)]
            left = jnp.concatenate([x[one] for one in parts], axis=1)
            right = jnp.concatenate(
                [
                    jnp.concatenate(
                        [half[s * 3 * w:(s + 1) * 3 * w, one] for one in parts], axis=0
                    )
                    for s in range(nz)
                ],
                axis=1,
            )
            total += jnp.dot(left, right, preferred_element_type=jnp.float32)
        return total

    acc[...] = sum(part(step) for step in range(count // depth))


def inner_kernel(where, held, weights, *refs):
    *before, out, acc = refs
    nz, w, _ = out.shape[1:]
    for i in range(QUADS - 2):
        products([(held, (i + t,)) for t in range(3)], weights[i + 1], acc, nz)
        for s in range(nz):
            total = acc[:, s * w:(s + 1) * w]
            out[i, s] = total + before[0][i, s] if before else total


def edge_kernel(kind, has_before, where, held, outside, weights, *refs):
    *refs, acc = refs
    core = where[3]
    last = (1 - core) if kind == "beside" else core
    base = last * (QUADS - 2)
    nz, w = refs[-1].shape[-3], refs[-1].shape[-1]
    tiles = [(held, (base,)), (held, (base + 1,)), (outside, ())]
    products(tiles, weights[last * (QUADS - 1)], acc, nz)

    def total(s):
        value = acc[:, s * w:(s + 1) * w]
        return value + refs[0][s] if has_before else value

    done = refs[1:] if has_before else refs
    if len(done) == 1:
        for s in range(nz):
            done[0][s] = total(s)
        return
    inner, beside, *homes = done
    quad = where[2]
    for v, home in enumerate(homes):
        for k in range(2):
            owner = ((v ^ (quad & 1)) << 1) + k

            @pl.when((owner == 1) | (owner == 2))
            def _():
                home[k] = inner[owner - 1]

            @pl.when(owner == last * (QUADS - 1))
            def _():
                for s in range(nz):
                    home[k, s] = total(s)

            @pl.when(owner == (1 - last) * (QUADS - 1))
            def _():
                home[k] = beside[...]


def ladder(kind, where, held, outside, weights, nz, before=None, done=()):
    w = held.shape[-1]
    before = [] if before is None else [before]
    shape = jax.ShapeDtypeStruct((nz, w, w), jnp.float32)
    if kind == "inner":
        kernel, shape = inner_kernel, jax.ShapeDtypeStruct((2, nz, w, w), jnp.float32)
    else:
        kernel = functools.partial(edge_kernel, kind, len(before) > 0)
    if done:
        shape = [jax.ShapeDtypeStruct((2, nz, w, w), jnp.float32)] * 2
    args = [held] + list(outside) + [weights] + before + list(done)
    return pl.pallas_call(
        kernel,
        out_shape=shape,
        in_specs=[SMEM] + [VMEM] * len(args),
        out_specs=[VMEM] * 2 if done else VMEM,
        scratch_shapes=[pltpu.VMEM((w, nz * w), jnp.float32)],
        compiler_params=pltpu.CompilerParams(vmem_limit_bytes=LIMIT),
        cost_estimate=FREE,
        name=kind,
    )(where, *args)


def body(factors, amplitudes, left_step, right_step, amp_owner, amp_slot):
    tiles = lax.axis_size("tile")
    here = lax.axis_index("tile")
    nz, w, _ = amplitudes.shape
    terms = left_step.shape[1]
    layers = tiles // GROUP
    layer, local = here >> 3, here & (GROUP - 1)
    quad, core = local >> 1, local & 1
    where = jnp.stack([layer, local, quad, core, here, tiles]).astype(jnp.int32)
    count = factors.shape[1] // QUADS
    pieces = PIECES if count % PIECES == 0 else 1
    size = count // pieces

    def send(value, target):
        pairs = []
        for z in range(layers):
            for s in range(GROUP):
                to = target(z, s // 2, s % 2)
                if to is not None and to != (z, s // 2, s % 2):
                    pairs.append((z * GROUP + s, to[0] * GROUP + to[1] * 2 + to[2]))
        return lax.ppermute(value, "tile", pairs)

    def cut(piece, t):
        start = (t ^ (local & 3)) * count + piece * size
        return lax.dynamic_slice_in_dim(factors[0], start, size, axis=0)

    def spread(part, t):
        return send(part, lambda z, q, k: (z, t ^ ((q & 1) * 2 + k), q >> 1))

    def to_core(value):
        return send(value, lambda z, q, k: (z, q, 1 - k))

    load = pack(tiles, amplitudes, left_step, right_step, amp_owner, amp_slot)
    where, load = lax.optimization_barrier((where, load))
    loads = [load] + [send(load, lambda z, q, k: (z, q ^ t, k)) for t in range(1, QUADS)]
    own = [[cut(piece, t) for t in range(QUADS)] for piece in range(pieces)]
    loads, own = lax.optimization_barrier((loads, own))
    parts = [{t: spread(own[0][t], t) for t in ORDER[:2]}]
    load = join(loads)
    turns = [
        send(load, lambda z, q, k: ((z + turn) % layers, q, k)) for turn in range(1, layers)
    ]
    sibling = to_core(load)
    if layers > 1:
        turns[0], sibling, own = lax.optimization_barrier((turns[0], sibling, own))
    for t in ORDER[2:]:
        parts[0][t] = spread(own[0][t], t)
    for piece in range(1, pieces):
        parts.append({t: spread(own[piece][t], t) for t in ORDER})
    mine = join([load] + turns)
    mine, parts[0] = lax.optimization_barrier((mine, parts[0]))
    other = to_core(mine)
    half = mix(where, mine, sibling, mine, nz, terms, layers)
    half, parts[0] = lax.optimization_barrier((half, parts[0]))
    weights = mix(where, mine, other, other, nz, terms, layers, (half,))

    def halves(parts, own):
        held, mid, halo = sort(where, [parts[t] for t in range(QUADS)], own)
        halo = send(
            halo,
            lambda z, q, k: (z + 2 * k - 1, q, 1 - k) if 0 <= z + 2 * k - 1 < layers else None,
        )
        return held, to_core(mid), halo

    held, mid, halo = halves(parts[0], own[0])
    ahead = list(ORDER) if pieces > 1 else []
    for t in ahead[:1]:
        held, parts[1][t] = lax.optimization_barrier((held, parts[1][t]))
    inner = beside = beyond = None
    for piece in range(pieces):
        last = piece == pieces - 1
        inner = ladder("inner", where, held, [], weights, nz, inner)
        mid, inner = lax.optimization_barrier((mid, inner))
        for t in ahead[1:2] if piece == 0 else []:
            mid, parts[1][t] = lax.optimization_barrier((mid, parts[1][t]))
        beside = ladder("beside", where, held, [mid], weights, nz, beside)
        halo, beside = lax.optimization_barrier((halo, beside))
        now, outside = held, halo
        if not last:
            beside, after = lax.optimization_barrier((beside, parts[piece + 1]))
            held, mid, halo = halves(after, own[piece + 1])
            held, outside = lax.optimization_barrier((held, outside))
        beyond = ladder(
            "beyond", where, now, [outside], weights, nz, beyond, (inner, beside) if last else ()
        )
        if not last:
            held, beyond = lax.optimization_barrier((held, beyond))

    stays = (quad >> 1) == core
    pair = jnp.where(stays, beyond[0], 0.0)
    for v in range(2):
        pair = pair + send(beyond[v], lambda z, q, k: (z, 2 * k + (v ^ (q & 1)), q >> 1))
    keep = jnp.where(core == 0, pair[0], pair[1])
    give = jnp.where(core == 0, pair[1], pair[0])
    total = keep + to_core(give)
    return lax.psum_scatter(total, "fit", scatter_dimension=1, tiled=True).astype(jnp.bfloat16)


def solution(mesh):
    return jax.shard_map(
        body,
        mesh=mesh,
        in_specs=(
            P("tile", "fit", None, None),
            P("tile", None, None),
            P("tile", None),
            P("tile", None),
            P("tile", None),
            P("tile", None),
        ),
        out_specs=P("tile", "fit", None),
        check_vma=False,
    )
```

```python
import functools

import jax
import jax.numpy as jnp
from jax import lax
from jax.experimental import pallas as pl
from jax.experimental.pallas import tpu as pltpu
from jax.sharding import PartitionSpec as P

GROUP = 8
QUADS = 4
SHARE = 0.625
ORDER = (0, 3, 1, 2)
ROWS = 16
DEPTH = 24
LIMIT = 32 * 1024 * 1024
SMALL = 6 * 1024 * 1024
VMEM = pl.BlockSpec(memory_space=pltpu.VMEM)
SMEM = pl.BlockSpec(memory_space=pltpu.SMEM)
NT = (((1,), (1,)), ((), ()))
FREE = pl.CostEstimate(flops=0, bytes_accessed=0, transcendentals=0)


def pack_kernel(tiles, *refs):
    *sources, out, rows, amps, left, right, owner, slot, sems = refs
    here = lax.axis_index("tile")
    copies = [
        pltpu.make_async_copy(source, held, sems.at[i])
        for i, (source, held) in enumerate(zip(sources, (amps, left, right, owner, slot)))
    ]
    for copy in copies:
        copy.start()
    nz, w, _ = amps.shape
    terms = owner.shape[1]
    rows[...] = jnp.zeros_like(rows)
    for copy in copies:
        copy.wait()
    left_at = jnp.clip(here + left[...], 0, tiles - 1) - here + 1
    right_at = jnp.clip(here + right[...], 0, tiles - 1) - here + 1
    first = lax.broadcasted_iota(jnp.int32, (nz, terms), 0) * 9
    place = first + left_at * 3 + right_at
    turned = first + jnp.where(left_at == 0, 2, left_at - 1) * 3
    turned = turned + jnp.where(right_at == 0, 2, right_at - 1)
    for i, value in enumerate((owner[...], slot[...], place, turned)):
        rows[i * nz:(i + 1) * nz, 0:terms] = value.astype(jnp.float32)
    for s in range(nz):
        out[0, s * w:(s + 1) * w] = amps[s]
    out[0, nz * w:] = rows[...].astype(out.dtype)


def pack(tiles, *sources):
    nz, w, _ = sources[0].shape
    return pl.pallas_call(
        functools.partial(pack_kernel, tiles),
        out_shape=jax.ShapeDtypeStruct((1, nz * w + ROWS, w), sources[0].dtype),
        in_specs=[pl.BlockSpec(memory_space=pl.ANY)] * len(sources),
        out_specs=VMEM,
        scratch_shapes=[pltpu.VMEM((ROWS, w), jnp.float32)]
        + [pltpu.VMEM(source.shape, source.dtype) for source in sources]
        + [pltpu.SemaphoreType.DMA((len(sources),))],
        compiler_params=pltpu.CompilerParams(vmem_limit_bytes=60 * 1024 * 1024),
        cost_estimate=FREE,
        name="pack",
    )(*sources)


def mix_kernel(terms, layers, where, lists_mine, lists_other, amps, *refs):
    *before, out, acc, rows, lists, sem = refs
    column = 1 if before else 0
    w = amps.shape[2]
    nz = acc.shape[0] // 9
    lines = rows.shape[0] // GROUP
    layer, local, core = where[0], where[1], where[3]

    for n, source in enumerate((lists_mine, lists_other)):
        for i in range(QUADS):
            listed = source[i, nz * w:nz * w + ROWS, :].astype(jnp.float32)
            at = (n * QUADS + i) * lines
            rows[at:at + lines] = listed[:lines].astype(jnp.int32)
    copy = pltpu.make_async_copy(rows, lists, sem)
    copy.start()
    copy.wait()

    for step in range(QUADS):
        total = acc if before else out.at[step]
        total[...] = before[0][step] if before else jnp.zeros_like(acc)
        entry = (core * QUADS + step) ^ local
        row = ((entry & 1) * QUADS + (entry >> 1)) * lines

        def add(i, carry):
            for s in range(nz):
                owner = lists[row + s, i]
                slot = lists[row + nz + s, i]
                place = lists[row + (3 if step == 0 else 2) * nz + s, i]
                away = (owner & (GROUP - 1)) ^ local
                turn = layer - (owner >> 3) + layers
                if layers & (layers - 1) == 0:
                    turn = turn & (layers - 1)
                else:
                    turn = lax.rem(turn, layers)
                part = pl.ds(pl.multiple_of(slot * w, w), w)

                @pl.when((away & 1) == column)
                def _():
                    tile = amps[turn * QUADS + (away >> 1), part, :]
                    total[place] = total[place] + tile.astype(jnp.float32)

            return carry

        lax.fori_loop(0, terms, add, 0)
        if not before:
            continue
        for s in range(nz):
            for l in range(3):
                for r in range(3):
                    out[step, (s * 3 + l) * w:(s * 3 + l + 1) * w, r * w:(r + 1) * w] = acc[
                        (s * 3 + l) * 3 + r
                    ].astype(out.dtype)


def mix(where, mine, other, amps, nz, terms, layers, before=()):
    w = amps.shape[2]
    lines = -(-4 * nz // 8) * 8
    first = jax.ShapeDtypeStruct((QUADS, 9 * nz, w, w), jnp.float32)
    second = jax.ShapeDtypeStruct((QUADS, 3 * w * nz, 3 * w), amps.dtype)
    return pl.pallas_call(
        functools.partial(mix_kernel, terms, layers),
        out_shape=second if before else first,
        in_specs=[SMEM] + [VMEM] * (3 + len(before)),
        out_specs=VMEM,
        scratch_shapes=[
            pltpu.VMEM((9 * nz, w, w), jnp.float32),
            pltpu.VMEM((GROUP * lines, w), jnp.int32),
            pltpu.SMEM((GROUP * lines, w), jnp.int32),
            pltpu.SemaphoreType.DMA,
        ],
        compiler_params=pltpu.CompilerParams(vmem_limit_bytes=SMALL),
        cost_estimate=FREE,
        name="mix",
    )(where, mine, other, amps, *before)


def join_kernel(*refs):
    *pieces, out = refs
    size = pieces[0].shape[0]
    for i, piece in enumerate(pieces):
        out[i * size:(i + 1) * size] = piece[...]


def join(pieces):
    size, *rest = pieces[0].shape
    return pl.pallas_call(
        join_kernel,
        out_shape=jax.ShapeDtypeStruct((len(pieces) * size, *rest), pieces[0].dtype),
        in_specs=[VMEM] * len(pieces),
        out_specs=VMEM,
        cost_estimate=FREE,
        compiler_params=pltpu.CompilerParams(vmem_limit_bytes=SMALL),
        name="join",
    )(*pieces)


def sort_kernel(where, a, b, c, d, own_a, own_d, held, mid, halo):
    quad, core = where[2], where[3]
    for t, (tile, own) in enumerate(((a, own_a), (b, None), (c, None), (d, own_d))):
        at = quad ^ t

        def lay(tile, use):
            for_mid = (at == 0) == (core == 1)

            @pl.when(use)
            def _():
                held[at] = tile[...]

            rim = ((at == 0) | (at == QUADS - 1)) & use

            @pl.when(rim & for_mid)
            def _():
                mid[...] = tile[...]

            @pl.when(rim & jnp.logical_not(for_mid))
            def _():
                halo[...] = tile[...]

        if own is None:
            lay(tile, at >= 0)
        else:
            stays = core * QUADS + at == where[1]
            lay(own, stays)
            lay(tile, jnp.logical_not(stays))


def sort(where, tiles, own):
    kind = jax.ShapeDtypeStruct(tiles[0].shape, tiles[0].dtype)
    return pl.pallas_call(
        sort_kernel,
        out_shape=(jax.ShapeDtypeStruct((QUADS,) + kind.shape, kind.dtype), kind, kind),
        in_specs=[SMEM] + [VMEM] * (QUADS + 2),
        out_specs=(VMEM, VMEM, VMEM),
        compiler_params=pltpu.CompilerParams(vmem_limit_bytes=SMALL),
        cost_estimate=FREE,
        name="sort",
    )(where, *tiles, own[0], own[QUADS - 1])


def products(tiles, weights, acc, nz):
    count, w = tiles[0][0].shape[-3:-1]
    depth = next(d for d in range(min(DEPTH, count), 0, -1) if count % d == 0)
    pair = 2 if depth % 2 == 0 else 1

    def part(step):
        rows = slice(step * depth, (step + 1) * depth)
        x = jnp.concatenate(
            [ref[lead + (rows,)].reshape(depth * w, w) for ref, lead in tiles], axis=1
        )
        half = lax.dot_general(weights, x, NT, preferred_element_type=jnp.float32)
        half = half.astype(x.dtype)
        total = jnp.zeros((w, nz * w), jnp.float32)
        for p in range(0, depth, pair):
            parts = [slice((p + i) * w, (p + i + 1) * w) for i in range(pair)]
            left = jnp.concatenate([x[one] for one in parts], axis=1)
            right = jnp.concatenate(
                [
                    jnp.concatenate(
                        [half[s * 3 * w:(s + 1) * 3 * w, one] for one in parts], axis=0
                    )
                    for s in range(nz)
                ],
                axis=1,
            )
            total += jnp.dot(left, right, preferred_element_type=jnp.float32)
        return total

    acc[...] = sum(part(step) for step in range(count // depth))


def inner_kernel(where, held, weights, *refs):
    *before, out, acc = refs
    nz, w, _ = out.shape[1:]
    for i in range(QUADS - 2):
        products([(held, (i + t,)) for t in range(3)], weights[i + 1], acc, nz)
        for s in range(nz):
            total = acc[:, s * w:(s + 1) * w]
            out[i, s] = total + before[0][i, s] if before else total


def edge_kernel(kind, has_before, where, held, outside, weights, *refs):
    *refs, acc = refs
    core = where[3]
    last = (1 - core) if kind == "beside" else core
    base = last * (QUADS - 2)
    nz, w = refs[-1].shape[-3], refs[-1].shape[-1]
    tiles = [(held, (base,)), (held, (base + 1,)), (outside, ())]
    products(tiles, weights[last * (QUADS - 1)], acc, nz)

    def total(s):
        value = acc[:, s * w:(s + 1) * w]
        return value + refs[0][s] if has_before else value

    done = refs[1:] if has_before else refs
    if len(done) == 1:
        for s in range(nz):
            done[0][s] = total(s)
        return
    inner, beside, *homes = done
    quad = where[2]
    for v, home in enumerate(homes):
        for k in range(2):
            owner = ((v ^ (quad & 1)) << 1) + k

            @pl.when((owner == 1) | (owner == 2))
            def _():
                home[k] = inner[owner - 1]

            @pl.when(owner == last * (QUADS - 1))
            def _():
                for s in range(nz):
                    home[k, s] = total(s)

            @pl.when(owner == (1 - last) * (QUADS - 1))
            def _():
                home[k] = beside[...]


def ladder(kind, where, held, outside, weights, nz, before=None, done=()):
    w = held.shape[-1]
    before = [] if before is None else [before]
    shape = jax.ShapeDtypeStruct((nz, w, w), jnp.float32)
    if kind == "inner":
        kernel, shape = inner_kernel, jax.ShapeDtypeStruct((2, nz, w, w), jnp.float32)
    else:
        kernel = functools.partial(edge_kernel, kind, len(before) > 0)
    if done:
        shape = [jax.ShapeDtypeStruct((2, nz, w, w), jnp.float32)] * 2
    args = [held] + list(outside) + [weights] + before + list(done)
    return pl.pallas_call(
        kernel,
        out_shape=shape,
        in_specs=[SMEM] + [VMEM] * len(args),
        out_specs=[VMEM] * 2 if done else VMEM,
        scratch_shapes=[pltpu.VMEM((w, nz * w), jnp.float32)],
        compiler_params=pltpu.CompilerParams(vmem_limit_bytes=LIMIT),
        cost_estimate=FREE,
        name=kind,
    )(where, *args)


def body(factors, amplitudes, left_step, right_step, amp_owner, amp_slot):
    tiles = lax.axis_size("tile")
    here = lax.axis_index("tile")
    nz, w, _ = amplitudes.shape
    terms = left_step.shape[1]
    layers = tiles // GROUP
    layer, local = here >> 3, here & (GROUP - 1)
    quad, core = local >> 1, local & 1
    where = jnp.stack([layer, local, quad, core, here, tiles]).astype(jnp.int32)
    count = factors.shape[1] // QUADS
    sizes = [int(count * SHARE)]
    sizes = [sizes[0], count - sizes[0]] if 0 < sizes[0] < count else [count]
    pieces = len(sizes)

    def send(value, target):
        pairs = []
        for z in range(layers):
            for s in range(GROUP):
                to = target(z, s // 2, s % 2)
                if to is not None and to != (z, s // 2, s % 2):
                    pairs.append((z * GROUP + s, to[0] * GROUP + to[1] * 2 + to[2]))
        return lax.ppermute(value, "tile", pairs)

    def cut(piece, t):
        start = (t ^ (local & 3)) * count + sum(sizes[:piece])
        return lax.dynamic_slice_in_dim(factors[0], start, sizes[piece], axis=0)

    def spread(part, t):
        return send(part, lambda z, q, k: (z, t ^ ((q & 1) * 2 + k), q >> 1))

    def to_core(value):
        return send(value, lambda z, q, k: (z, q, 1 - k))

    load = pack(tiles, amplitudes, left_step, right_step, amp_owner, amp_slot)
    where, load = lax.optimization_barrier((where, load))
    loads = [load] + [send(load, lambda z, q, k: (z, q ^ t, k)) for t in range(1, QUADS)]
    own = [[cut(piece, t) for t in range(QUADS)] for piece in range(pieces)]
    loads, own = lax.optimization_barrier((loads, own))
    parts = [{t: spread(own[0][t], t) for t in ORDER[:2]}]
    load = join(loads)
    turns = [
        send(load, lambda z, q, k: ((z + turn) % layers, q, k)) for turn in range(1, layers)
    ]
    sibling = to_core(load)
    if layers > 1:
        turns[0], sibling, own = lax.optimization_barrier((turns[0], sibling, own))
    for t in ORDER[2:]:
        parts[0][t] = spread(own[0][t], t)
    for piece in range(1, pieces):
        parts.append({t: spread(own[piece][t], t) for t in ORDER})
    mine = join([load] + turns)
    for t in ORDER[:3]:
        mine, parts[0][t] = lax.optimization_barrier((mine, parts[0][t]))
    other = to_core(mine)
    half = mix(where, mine, sibling, mine, nz, terms, layers)
    weights = mix(where, mine, other, other, nz, terms, layers, (half,))
    for t in ORDER[3:]:
        weights, parts[0][t] = lax.optimization_barrier((weights, parts[0][t]))

    def halves(parts, own):
        held, mid, halo = sort(where, [parts[t] for t in range(QUADS)], own)
        halo = send(
            halo,
            lambda z, q, k: (z + 2 * k - 1, q, 1 - k) if 0 <= z + 2 * k - 1 < layers else None,
        )
        return held, to_core(mid), halo

    held, mid, halo = halves(parts[0], own[0])
    ahead = list(ORDER) if pieces > 1 else []
    for t in ahead[:1]:
        held, parts[1][t] = lax.optimization_barrier((held, parts[1][t]))
    inner = beside = beyond = None
    for piece in range(pieces):
        last = piece == pieces - 1
        inner = ladder("inner", where, held, [], weights, nz, inner)
        mid, inner = lax.optimization_barrier((mid, inner))
        for t in ahead[1:2] if piece == 0 else []:
            mid, parts[1][t] = lax.optimization_barrier((mid, parts[1][t]))
        beside = ladder("beside", where, held, [mid], weights, nz, beside)
        halo, beside = lax.optimization_barrier((halo, beside))
        now, outside = held, halo
        if not last:
            beside, after = lax.optimization_barrier((beside, parts[piece + 1]))
            held, mid, halo = halves(after, own[piece + 1])
            held, outside = lax.optimization_barrier((held, outside))
        beyond = ladder(
            "beyond", where, now, [outside], weights, nz, beyond, (inner, beside) if last else ()
        )
        if not last:
            held, beyond = lax.optimization_barrier((held, beyond))

    stays = (quad >> 1) == core
    pair = jnp.where(stays, beyond[0], 0.0)
    for v in range(2):
        pair = pair + send(beyond[v], lambda z, q, k: (z, 2 * k + (v ^ (q & 1)), q >> 1))
    keep = jnp.where(core == 0, pair[0], pair[1])
    give = jnp.where(core == 0, pair[1], pair[0])
    total = keep + to_core(give)
    return lax.psum_scatter(total, "fit", scatter_dimension=1, tiled=True).astype(jnp.bfloat16)


def solution(mesh):
    return jax.shard_map(
        body,
        mesh=mesh,
        in_specs=(
            P("tile", "fit", None, None),
            P("tile", None, None),
            P("tile", None),
            P("tile", None),
            P("tile", None),
            P("tile", None),
        ),
        out_specs=P("tile", "fit", None),
        check_vma=False,
    )
```

```python
import functools

import jax
import jax.numpy as jnp
from jax import lax
from jax.experimental import pallas as pl
from jax.experimental.pallas import tpu as pltpu
from jax.sharding import PartitionSpec as P

GROUP = 8
QUADS = 4
SHARE = 0.5
ORDER = (0, 3, 1, 2)
ROWS = 16
DEPTH = 16
LIMIT = 32 * 1024 * 1024
SMALL = 6 * 1024 * 1024
VMEM = pl.BlockSpec(memory_space=pltpu.VMEM)
SMEM = pl.BlockSpec(memory_space=pltpu.SMEM)
NT = (((1,), (1,)), ((), ()))
FREE = pl.CostEstimate(flops=0, bytes_accessed=0, transcendentals=0)


def pack_kernel(tiles, *refs):
    *sources, out, rows, amps, left, right, owner, slot, sems = refs
    here = lax.axis_index("tile")
    copies = [
        pltpu.make_async_copy(source, held, sems.at[i])
        for i, (source, held) in enumerate(zip(sources, (amps, left, right, owner, slot)))
    ]
    for copy in copies:
        copy.start()
    nz, w, _ = amps.shape
    terms = owner.shape[1]
    rows[...] = jnp.zeros_like(rows)
    for copy in copies:
        copy.wait()
    left_at = jnp.clip(here + left[...], 0, tiles - 1) - here + 1
    right_at = jnp.clip(here + right[...], 0, tiles - 1) - here + 1
    first = lax.broadcasted_iota(jnp.int32, (nz, terms), 0) * 9
    place = first + left_at * 3 + right_at
    turned = first + jnp.where(left_at == 0, 2, left_at - 1) * 3
    turned = turned + jnp.where(right_at == 0, 2, right_at - 1)
    for i, value in enumerate((owner[...], slot[...], place, turned)):
        rows[i * nz:(i + 1) * nz, 0:terms] = value.astype(jnp.float32)
    for s in range(nz):
        out[0, s * w:(s + 1) * w] = amps[s]
    out[0, nz * w:] = rows[...].astype(out.dtype)


def pack(tiles, *sources):
    nz, w, _ = sources[0].shape
    return pl.pallas_call(
        functools.partial(pack_kernel, tiles),
        out_shape=jax.ShapeDtypeStruct((1, nz * w + ROWS, w), sources[0].dtype),
        in_specs=[pl.BlockSpec(memory_space=pl.ANY)] * len(sources),
        out_specs=VMEM,
        scratch_shapes=[pltpu.VMEM((ROWS, w), jnp.float32)]
        + [pltpu.VMEM(source.shape, source.dtype) for source in sources]
        + [pltpu.SemaphoreType.DMA((len(sources),))],
        compiler_params=pltpu.CompilerParams(vmem_limit_bytes=60 * 1024 * 1024),
        cost_estimate=FREE,
        name="pack",
    )(*sources)


def mix_kernel(terms, layers, where, lists_mine, lists_other, amps, *refs):
    *before, out, acc, rows, lists, sem = refs
    column = 1 if before else 0
    w = amps.shape[2]
    nz = acc.shape[0] // 9
    lines = rows.shape[0] // GROUP
    layer, local, core = where[0], where[1], where[3]

    for n, source in enumerate((lists_mine, lists_other)):
        for i in range(QUADS):
            listed = source[i, nz * w:nz * w + ROWS, :].astype(jnp.float32)
            at = (n * QUADS + i) * lines
            rows[at:at + lines] = listed[:lines].astype(jnp.int32)
    copy = pltpu.make_async_copy(rows, lists, sem)
    copy.start()
    copy.wait()

    for step in range(QUADS):
        total = acc if before else out.at[step]
        total[...] = before[0][step] if before else jnp.zeros_like(acc)
        entry = (core * QUADS + step) ^ local
        row = ((entry & 1) * QUADS + (entry >> 1)) * lines

        def add(i, carry):
            for s in range(nz):
                owner = lists[row + s, i]
                slot = lists[row + nz + s, i]
                place = lists[row + (3 if step == 0 else 2) * nz + s, i]
                away = (owner & (GROUP - 1)) ^ local
                turn = layer - (owner >> 3) + layers
                if layers & (layers - 1) == 0:
                    turn = turn & (layers - 1)
                else:
                    turn = lax.rem(turn, layers)
                part = pl.ds(pl.multiple_of(slot * w, w), w)

                @pl.when((away & 1) == column)
                def _():
                    tile = amps[turn * QUADS + (away >> 1), part, :]
                    total[place] = total[place] + tile.astype(jnp.float32)

            return carry

        lax.fori_loop(0, terms, add, 0)
        if not before:
            continue
        for s in range(nz):
            for l in range(3):
                for r in range(3):
                    out[step, (s * 3 + l) * w:(s * 3 + l + 1) * w, r * w:(r + 1) * w] = acc[
                        (s * 3 + l) * 3 + r
                    ].astype(out.dtype)


def mix(where, mine, other, amps, nz, terms, layers, before=()):
    w = amps.shape[2]
    lines = -(-4 * nz // 8) * 8
    first = jax.ShapeDtypeStruct((QUADS, 9 * nz, w, w), jnp.float32)
    second = jax.ShapeDtypeStruct((QUADS, 3 * w * nz, 3 * w), amps.dtype)
    return pl.pallas_call(
        functools.partial(mix_kernel, terms, layers),
        out_shape=second if before else first,
        in_specs=[SMEM] + [VMEM] * (3 + len(before)),
        out_specs=VMEM,
        scratch_shapes=[
            pltpu.VMEM((9 * nz, w, w), jnp.float32),
            pltpu.VMEM((GROUP * lines, w), jnp.int32),
            pltpu.SMEM((GROUP * lines, w), jnp.int32),
            pltpu.SemaphoreType.DMA,
        ],
        compiler_params=pltpu.CompilerParams(vmem_limit_bytes=SMALL),
        cost_estimate=FREE,
        name="mix",
    )(where, mine, other, amps, *before)


def join_kernel(*refs):
    *pieces, out = refs
    size = pieces[0].shape[0]
    for i, piece in enumerate(pieces):
        out[i * size:(i + 1) * size] = piece[...]


def join(pieces):
    size, *rest = pieces[0].shape
    return pl.pallas_call(
        join_kernel,
        out_shape=jax.ShapeDtypeStruct((len(pieces) * size, *rest), pieces[0].dtype),
        in_specs=[VMEM] * len(pieces),
        out_specs=VMEM,
        cost_estimate=FREE,
        compiler_params=pltpu.CompilerParams(vmem_limit_bytes=SMALL),
        name="join",
    )(*pieces)


def sort_kernel(where, a, b, c, d, own_a, own_d, held, mid, halo):
    quad, core = where[2], where[3]
    for t, (tile, own) in enumerate(((a, own_a), (b, None), (c, None), (d, own_d))):
        at = quad ^ t

        def lay(tile, use):
            for_mid = (at == 0) == (core == 1)

            @pl.when(use)
            def _():
                held[at] = tile[...]

            rim = ((at == 0) | (at == QUADS - 1)) & use

            @pl.when(rim & for_mid)
            def _():
                mid[...] = tile[...]

            @pl.when(rim & jnp.logical_not(for_mid))
            def _():
                halo[...] = tile[...]

        if own is None:
            lay(tile, at >= 0)
        else:
            stays = core * QUADS + at == where[1]
            lay(own, stays)
            lay(tile, jnp.logical_not(stays))


def sort(where, tiles, own):
    kind = jax.ShapeDtypeStruct(tiles[0].shape, tiles[0].dtype)
    return pl.pallas_call(
        sort_kernel,
        out_shape=(jax.ShapeDtypeStruct((QUADS,) + kind.shape, kind.dtype), kind, kind),
        in_specs=[SMEM] + [VMEM] * (QUADS + 2),
        out_specs=(VMEM, VMEM, VMEM),
        compiler_params=pltpu.CompilerParams(vmem_limit_bytes=SMALL),
        cost_estimate=FREE,
        name="sort",
    )(where, *tiles, own[0], own[QUADS - 1])


def products(tiles, weights, acc, nz):
    count, w = tiles[0][0].shape[-3:-1]
    depth = next(d for d in range(min(DEPTH, count), 0, -1) if count % d == 0)
    pair = 2 if depth % 2 == 0 else 1

    def part(step):
        rows = slice(step * depth, (step + 1) * depth)
        x = jnp.concatenate(
            [ref[lead + (rows,)].reshape(depth * w, w) for ref, lead in tiles], axis=1
        )
        half = lax.dot_general(weights, x, NT, preferred_element_type=jnp.float32)
        half = half.astype(x.dtype)
        total = jnp.zeros((w, nz * w), jnp.float32)
        for p in range(0, depth, pair):
            parts = [slice((p + i) * w, (p + i + 1) * w) for i in range(pair)]
            left = jnp.concatenate([x[one] for one in parts], axis=1)
            right = jnp.concatenate(
                [
                    jnp.concatenate(
                        [half[s * 3 * w:(s + 1) * 3 * w, one] for one in parts], axis=0
                    )
                    for s in range(nz)
                ],
                axis=1,
            )
            total += jnp.dot(left, right, preferred_element_type=jnp.float32)
        return total

    acc[...] = sum(part(step) for step in range(count // depth))


def inner_kernel(where, held, weights, *refs):
    *before, out, acc = refs
    nz, w, _ = out.shape[1:]
    for i in range(QUADS - 2):
        products([(held, (i + t,)) for t in range(3)], weights[i + 1], acc, nz)
        for s in range(nz):
            total = acc[:, s * w:(s + 1) * w]
            out[i, s] = total + before[0][i, s] if before else total


def edge_kernel(kind, has_before, where, held, outside, weights, *refs):
    *refs, acc = refs
    core = where[3]
    last = (1 - core) if kind == "beside" else core
    base = last * (QUADS - 2)
    nz, w = refs[-1].shape[-3], refs[-1].shape[-1]
    tiles = [(held, (base,)), (held, (base + 1,)), (outside, ())]
    products(tiles, weights[last * (QUADS - 1)], acc, nz)

    def total(s):
        value = acc[:, s * w:(s + 1) * w]
        return value + refs[0][s] if has_before else value

    done = refs[1:] if has_before else refs
    if len(done) == 1:
        for s in range(nz):
            done[0][s] = total(s)
        return
    inner, beside, *homes = done
    quad = where[2]
    for v, home in enumerate(homes):
        for k in range(2):
            owner = ((v ^ (quad & 1)) << 1) + k

            @pl.when((owner == 1) | (owner == 2))
            def _():
                home[k] = inner[owner - 1]

            @pl.when(owner == last * (QUADS - 1))
            def _():
                for s in range(nz):
                    home[k, s] = total(s)

            @pl.when(owner == (1 - last) * (QUADS - 1))
            def _():
                home[k] = beside[...]


def ladder(kind, where, held, outside, weights, nz, before=None, done=()):
    w = held.shape[-1]
    before = [] if before is None else [before]
    shape = jax.ShapeDtypeStruct((nz, w, w), jnp.float32)
    if kind == "inner":
        kernel, shape = inner_kernel, jax.ShapeDtypeStruct((2, nz, w, w), jnp.float32)
    else:
        kernel = functools.partial(edge_kernel, kind, len(before) > 0)
    if done:
        shape = [jax.ShapeDtypeStruct((2, nz, w, w), jnp.float32)] * 2
    args = [held] + list(outside) + [weights] + before + list(done)
    return pl.pallas_call(
        kernel,
        out_shape=shape,
        in_specs=[SMEM] + [VMEM] * len(args),
        out_specs=[VMEM] * 2 if done else VMEM,
        scratch_shapes=[pltpu.VMEM((w, nz * w), jnp.float32)],
        compiler_params=pltpu.CompilerParams(vmem_limit_bytes=LIMIT),
        cost_estimate=FREE,
        name=kind,
    )(where, *args)


def body(factors, amplitudes, left_step, right_step, amp_owner, amp_slot):
    tiles = lax.axis_size("tile")
    here = lax.axis_index("tile")
    nz, w, _ = amplitudes.shape
    terms = left_step.shape[1]
    layers = tiles // GROUP
    layer, local = here >> 3, here & (GROUP - 1)
    quad, core = local >> 1, local & 1
    where = jnp.stack([layer, local, quad, core, here, tiles]).astype(jnp.int32)
    count = factors.shape[1] // QUADS
    sizes = [int(count * SHARE)]
    sizes = [sizes[0], count - sizes[0]] if 0 < sizes[0] < count else [count]
    pieces = len(sizes)

    def send(value, target):
        pairs = []
        for z in range(layers):
            for s in range(GROUP):
                to = target(z, s // 2, s % 2)
                if to is not None and to != (z, s // 2, s % 2):
                    pairs.append((z * GROUP + s, to[0] * GROUP + to[1] * 2 + to[2]))
        return lax.ppermute(value, "tile", pairs)

    def cut(piece, t):
        start = (t ^ (local & 3)) * count + sum(sizes[:piece])
        return lax.dynamic_slice_in_dim(factors[0], start, sizes[piece], axis=0)

    def spread(part, t):
        return send(part, lambda z, q, k: (z, t ^ ((q & 1) * 2 + k), q >> 1))

    def to_core(value):
        return send(value, lambda z, q, k: (z, q, 1 - k))

    load = pack(tiles, amplitudes, left_step, right_step, amp_owner, amp_slot)
    where, load = lax.optimization_barrier((where, load))
    loads = [load] + [send(load, lambda z, q, k: (z, q ^ t, k)) for t in range(1, QUADS)]
    own = [[cut(piece, t) for t in range(QUADS)] for piece in range(pieces)]
    loads, own = lax.optimization_barrier((loads, own))
    parts = [{t: spread(own[0][t], t) for t in ORDER[:2]}]
    load = join(loads)
    turns = [
        send(load, lambda z, q, k: ((z + turn) % layers, q, k)) for turn in range(1, layers)
    ]
    sibling = to_core(load)
    if layers > 1:
        turns[0], sibling, own = lax.optimization_barrier((turns[0], sibling, own))
    for t in ORDER[2:]:
        parts[0][t] = spread(own[0][t], t)
    for piece in range(1, pieces):
        parts.append({t: spread(own[piece][t], t) for t in ORDER})
    mine = join([load] + turns)
    for t in ORDER[:3]:
        mine, parts[0][t] = lax.optimization_barrier((mine, parts[0][t]))
    other = to_core(mine)
    half = mix(where, mine, sibling, mine, nz, terms, layers)
    weights = mix(where, mine, other, other, nz, terms, layers, (half,))
    for t in ORDER[3:]:
        weights, parts[0][t] = lax.optimization_barrier((weights, parts[0][t]))

    def halves(parts, own):
        held, mid, halo = sort(where, [parts[t] for t in range(QUADS)], own)
        halo = send(
            halo,
            lambda z, q, k: (z + 2 * k - 1, q, 1 - k) if 0 <= z + 2 * k - 1 < layers else None,
        )
        return held, to_core(mid), halo

    held, mid, halo = halves(parts[0], own[0])
    ahead = list(ORDER) if pieces > 1 else []
    for t in ahead[:2]:
        held, parts[1][t] = lax.optimization_barrier((held, parts[1][t]))
    inner = beside = beyond = None
    for piece in range(pieces):
        last = piece == pieces - 1
        inner = ladder("inner", where, held, [], weights, nz, inner)
        mid, inner = lax.optimization_barrier((mid, inner))
        beside = ladder("beside", where, held, [mid], weights, nz, beside)
        halo, beside = lax.optimization_barrier((halo, beside))
        beyond = ladder(
            "beyond", where, held, [halo], weights, nz, beyond, (inner, beside) if last else ()
        )
        if not last:
            beyond, after = lax.optimization_barrier((beyond, parts[piece + 1]))
            held, mid, halo = halves(after, own[piece + 1])

    stays = (quad >> 1) == core
    pair = jnp.where(stays, beyond[0], 0.0)
    for v in range(2):
        pair = pair + send(beyond[v], lambda z, q, k: (z, 2 * k + (v ^ (q & 1)), q >> 1))
    keep = jnp.where(core == 0, pair[0], pair[1])
    give = jnp.where(core == 0, pair[1], pair[0])
    total = keep + to_core(give)
    return lax.psum_scatter(total, "fit", scatter_dimension=1, tiled=True).astype(jnp.bfloat16)


def solution(mesh):
    return jax.shard_map(
        body,
        mesh=mesh,
        in_specs=(
            P("tile", "fit", None, None),
            P("tile", None, None),
            P("tile", None),
            P("tile", None),
            P("tile", None),
            P("tile", None),
        ),
        out_specs=P("tile", "fit", None),
        check_vma=False,
    )
```

```python
import functools

import jax
import jax.numpy as jnp
from jax import lax
from jax.experimental import pallas as pl
from jax.experimental.pallas import tpu as pltpu
from jax.sharding import PartitionSpec as P

GROUP = 8
QUADS = 4
PIECES = 2
ORDER = (0, 3, 1, 2)
ROWS = 16
DEPTH = 16
LIMIT = 32 * 1024 * 1024
SMALL = 6 * 1024 * 1024
VMEM = pl.BlockSpec(memory_space=pltpu.VMEM)
SMEM = pl.BlockSpec(memory_space=pltpu.SMEM)
NT = (((1,), (1,)), ((), ()))
FREE = pl.CostEstimate(flops=0, bytes_accessed=0, transcendentals=0)


def pack_kernel(tiles, *refs):
    *sources, out, rows, amps, left, right, owner, slot, sems = refs
    here = lax.axis_index("tile")
    copies = [
        pltpu.make_async_copy(source, held, sems.at[i])
        for i, (source, held) in enumerate(zip(sources, (amps, left, right, owner, slot)))
    ]
    for copy in copies:
        copy.start()
    nz, w, _ = amps.shape
    terms = owner.shape[1]
    rows[...] = jnp.zeros_like(rows)
    for copy in copies:
        copy.wait()
    left_at = jnp.clip(here + left[...], 0, tiles - 1) - here + 1
    right_at = jnp.clip(here + right[...], 0, tiles - 1) - here + 1
    first = lax.broadcasted_iota(jnp.int32, (nz, terms), 0) * 9
    place = first + left_at * 3 + right_at
    turned = first + jnp.where(left_at == 0, 2, left_at - 1) * 3
    turned = turned + jnp.where(right_at == 0, 2, right_at - 1)
    for i, value in enumerate((owner[...], slot[...], place, turned)):
        rows[i * nz:(i + 1) * nz, 0:terms] = value.astype(jnp.float32)
    for s in range(nz):
        out[0, s * w:(s + 1) * w] = amps[s]
    out[0, nz * w:] = rows[...].astype(out.dtype)


def pack(tiles, *sources):
    nz, w, _ = sources[0].shape
    return pl.pallas_call(
        functools.partial(pack_kernel, tiles),
        out_shape=jax.ShapeDtypeStruct((1, nz * w + ROWS, w), sources[0].dtype),
        in_specs=[pl.BlockSpec(memory_space=pl.ANY)] * len(sources),
        out_specs=VMEM,
        scratch_shapes=[pltpu.VMEM((ROWS, w), jnp.float32)]
        + [pltpu.VMEM(source.shape, source.dtype) for source in sources]
        + [pltpu.SemaphoreType.DMA((len(sources),))],
        compiler_params=pltpu.CompilerParams(vmem_limit_bytes=60 * 1024 * 1024),
        cost_estimate=FREE,
        name="pack",
    )(*sources)


def mix_kernel(terms, layers, where, lists_mine, lists_other, amps, *refs):
    *before, out, acc, rows, lists, sem = refs
    column = 1 if before else 0
    w = amps.shape[2]
    nz = acc.shape[0] // 9
    lines = rows.shape[0] // GROUP
    layer, local, core = where[0], where[1], where[3]

    for n, source in enumerate((lists_mine, lists_other)):
        for i in range(QUADS):
            listed = source[i, nz * w:nz * w + ROWS, :].astype(jnp.float32)
            at = (n * QUADS + i) * lines
            rows[at:at + lines] = listed[:lines].astype(jnp.int32)
    copy = pltpu.make_async_copy(rows, lists, sem)
    copy.start()
    copy.wait()

    for step in range(QUADS):
        total = acc if before else out.at[step]
        total[...] = before[0][step] if before else jnp.zeros_like(acc)
        entry = (core * QUADS + step) ^ local
        row = ((entry & 1) * QUADS + (entry >> 1)) * lines

        def add(i, carry):
            for s in range(nz):
                owner = lists[row + s, i]
                slot = lists[row + nz + s, i]
                place = lists[row + (3 if step == 0 else 2) * nz + s, i]
                away = (owner & (GROUP - 1)) ^ local
                turn = layer - (owner >> 3) + layers
                if layers & (layers - 1) == 0:
                    turn = turn & (layers - 1)
                else:
                    turn = lax.rem(turn, layers)
                part = pl.ds(pl.multiple_of(slot * w, w), w)

                @pl.when((away & 1) == column)
                def _():
                    tile = amps[turn * QUADS + (away >> 1), part, :]
                    total[place] = total[place] + tile.astype(jnp.float32)

            return carry

        lax.fori_loop(0, terms, add, 0)
        if not before:
            continue
        for s in range(nz):
            for l in range(3):
                for r in range(3):
                    out[step, (s * 3 + l) * w:(s * 3 + l + 1) * w, r * w:(r + 1) * w] = acc[
                        (s * 3 + l) * 3 + r
                    ].astype(out.dtype)


def mix(where, mine, other, amps, nz, terms, layers, before=()):
    w = amps.shape[2]
    lines = -(-4 * nz // 8) * 8
    first = jax.ShapeDtypeStruct((QUADS, 9 * nz, w, w), jnp.float32)
    second = jax.ShapeDtypeStruct((QUADS, 3 * w * nz, 3 * w), amps.dtype)
    return pl.pallas_call(
        functools.partial(mix_kernel, terms, layers),
        out_shape=second if before else first,
        in_specs=[SMEM] + [VMEM] * (3 + len(before)),
        out_specs=VMEM,
        scratch_shapes=[
            pltpu.VMEM((9 * nz, w, w), jnp.float32),
            pltpu.VMEM((GROUP * lines, w), jnp.int32),
            pltpu.SMEM((GROUP * lines, w), jnp.int32),
            pltpu.SemaphoreType.DMA,
        ],
        compiler_params=pltpu.CompilerParams(vmem_limit_bytes=SMALL),
        cost_estimate=FREE,
        name="mix",
    )(where, mine, other, amps, *before)


def join_kernel(*refs):
    *pieces, out = refs
    size = pieces[0].shape[0]
    for i, piece in enumerate(pieces):
        out[i * size:(i + 1) * size] = piece[...]


def join(pieces):
    size, *rest = pieces[0].shape
    return pl.pallas_call(
        join_kernel,
        out_shape=jax.ShapeDtypeStruct((len(pieces) * size, *rest), pieces[0].dtype),
        in_specs=[VMEM] * len(pieces),
        out_specs=VMEM,
        cost_estimate=FREE,
        compiler_params=pltpu.CompilerParams(vmem_limit_bytes=SMALL),
        name="join",
    )(*pieces)


def sort_kernel(where, a, b, c, d, own_a, own_d, held, mid, halo):
    quad, core = where[2], where[3]
    for t, (tile, own) in enumerate(((a, own_a), (b, None), (c, None), (d, own_d))):
        at = quad ^ t

        def lay(tile, use):
            for_mid = (at == 0) == (core == 1)

            @pl.when(use)
            def _():
                held[at] = tile[...]

            rim = ((at == 0) | (at == QUADS - 1)) & use

            @pl.when(rim & for_mid)
            def _():
                mid[...] = tile[...]

            @pl.when(rim & jnp.logical_not(for_mid))
            def _():
                halo[...] = tile[...]

        if own is None:
            lay(tile, at >= 0)
        else:
            stays = core * QUADS + at == where[1]
            lay(own, stays)
            lay(tile, jnp.logical_not(stays))


def sort(where, tiles, own):
    kind = jax.ShapeDtypeStruct(tiles[0].shape, tiles[0].dtype)
    return pl.pallas_call(
        sort_kernel,
        out_shape=(jax.ShapeDtypeStruct((QUADS,) + kind.shape, kind.dtype), kind, kind),
        in_specs=[SMEM] + [VMEM] * (QUADS + 2),
        out_specs=(VMEM, VMEM, VMEM),
        compiler_params=pltpu.CompilerParams(vmem_limit_bytes=SMALL),
        cost_estimate=FREE,
        name="sort",
    )(where, *tiles, own[0], own[QUADS - 1])


def products(tiles, weights, acc, nz):
    count, w = tiles[0][0].shape[-3:-1]
    depth = next(d for d in (DEPTH, 8, 4, 2, 1) if count % d == 0)
    pair = 2 if depth % 2 == 0 else 1

    def part(step):
        rows = slice(step * depth, (step + 1) * depth)
        x = jnp.concatenate(
            [ref[lead + (rows,)].reshape(depth * w, w) for ref, lead in tiles], axis=1
        )
        half = lax.dot_general(weights, x, NT, preferred_element_type=jnp.float32)
        half = half.astype(x.dtype)
        total = jnp.zeros((w, nz * w), jnp.float32)
        for p in range(0, depth, pair):
            parts = [slice((p + i) * w, (p + i + 1) * w) for i in range(pair)]
            left = jnp.concatenate([x[one] for one in parts], axis=1)
            right = jnp.concatenate(
                [
                    jnp.concatenate(
                        [half[s * 3 * w:(s + 1) * 3 * w, one] for one in parts], axis=0
                    )
                    for s in range(nz)
                ],
                axis=1,
            )
            total += jnp.dot(left, right, preferred_element_type=jnp.float32)
        return total

    acc[...] = sum(part(step) for step in range(count // depth))


def inner_kernel(where, held, weights, *refs):
    *before, out, acc = refs
    nz, w, _ = out.shape[1:]
    for i in range(QUADS - 2):
        products([(held, (i + t,)) for t in range(3)], weights[i + 1], acc, nz)
        for s in range(nz):
            total = acc[:, s * w:(s + 1) * w]
            out[i, s] = total + before[0][i, s] if before else total


def edge_kernel(kind, has_before, where, held, outside, weights, *refs):
    *refs, acc = refs
    core = where[3]
    last = (1 - core) if kind == "beside" else core
    base = last * (QUADS - 2)
    nz, w = refs[-1].shape[-3], refs[-1].shape[-1]
    tiles = [(held, (base,)), (held, (base + 1,)), (outside, ())]
    products(tiles, weights[last * (QUADS - 1)], acc, nz)

    def total(s):
        value = acc[:, s * w:(s + 1) * w]
        return value + refs[0][s] if has_before else value

    done = refs[1:] if has_before else refs
    if len(done) == 1:
        for s in range(nz):
            done[0][s] = total(s)
        return
    inner, beside, *homes = done
    quad = where[2]
    for v, home in enumerate(homes):
        for k in range(2):
            owner = ((v ^ (quad & 1)) << 1) + k

            @pl.when((owner == 1) | (owner == 2))
            def _():
                home[k] = inner[owner - 1].astype(home.dtype)

            @pl.when(owner == last * (QUADS - 1))
            def _():
                for s in range(nz):
                    home[k, s] = total(s).astype(home.dtype)

            @pl.when(owner == (1 - last) * (QUADS - 1))
            def _():
                home[k] = beside[...].astype(home.dtype)


def ladder(kind, where, held, outside, weights, nz, before=None, done=()):
    w = held.shape[-1]
    before = [] if before is None else [before]
    shape = jax.ShapeDtypeStruct((nz, w, w), jnp.float32)
    if kind == "inner":
        kernel, shape = inner_kernel, jax.ShapeDtypeStruct((2, nz, w, w), jnp.float32)
    else:
        kernel = functools.partial(edge_kernel, kind, len(before) > 0)
    if done:
        shape = [jax.ShapeDtypeStruct((2, nz, w, w), held.dtype)] * 2
    args = [held] + list(outside) + [weights] + before + list(done)
    return pl.pallas_call(
        kernel,
        out_shape=shape,
        in_specs=[SMEM] + [VMEM] * len(args),
        out_specs=[VMEM] * 2 if done else VMEM,
        scratch_shapes=[pltpu.VMEM((w, nz * w), jnp.float32)],
        compiler_params=pltpu.CompilerParams(vmem_limit_bytes=LIMIT),
        cost_estimate=FREE,
        name=kind,
    )(where, *args)


def body(factors, amplitudes, left_step, right_step, amp_owner, amp_slot):
    tiles = lax.axis_size("tile")
    here = lax.axis_index("tile")
    nz, w, _ = amplitudes.shape
    terms = left_step.shape[1]
    layers = tiles // GROUP
    layer, local = here >> 3, here & (GROUP - 1)
    quad, core = local >> 1, local & 1
    where = jnp.stack([layer, local, quad, core, here, tiles]).astype(jnp.int32)
    count = factors.shape[1] // QUADS
    pieces = PIECES if count % PIECES == 0 else 1
    size = count // pieces

    def send(value, target):
        pairs = []
        for z in range(layers):
            for s in range(GROUP):
                to = target(z, s // 2, s % 2)
                if to is not None and to != (z, s // 2, s % 2):
                    pairs.append((z * GROUP + s, to[0] * GROUP + to[1] * 2 + to[2]))
        return lax.ppermute(value, "tile", pairs)

    def cut(piece, t):
        start = (t ^ (local & 3)) * count + piece * size
        return lax.dynamic_slice_in_dim(factors[0], start, size, axis=0)

    def spread(part, t):
        return send(part, lambda z, q, k: (z, t ^ ((q & 1) * 2 + k), q >> 1))

    def to_core(value):
        return send(value, lambda z, q, k: (z, q, 1 - k))

    load = pack(tiles, amplitudes, left_step, right_step, amp_owner, amp_slot)
    where, load = lax.optimization_barrier((where, load))
    loads = [load] + [send(load, lambda z, q, k: (z, q ^ t, k)) for t in range(1, QUADS)]
    own = [[cut(piece, t) for t in range(QUADS)] for piece in range(pieces)]
    loads, own = lax.optimization_barrier((loads, own))
    parts = [{t: spread(own[0][t], t) for t in ORDER[:2]}]
    load = join(loads)
    turns = [
        send(load, lambda z, q, k: ((z + turn) % layers, q, k)) for turn in range(1, layers)
    ]
    sibling = to_core(load)
    if layers > 1:
        turns[0], sibling, own = lax.optimization_barrier((turns[0], sibling, own))
    for t in ORDER[2:]:
        parts[0][t] = spread(own[0][t], t)
    for piece in range(1, pieces):
        parts.append({t: spread(own[piece][t], t) for t in ORDER})
    mine = join([load] + turns)
    mine, parts[0] = lax.optimization_barrier((mine, parts[0]))
    other = to_core(mine)
    half = mix(where, mine, sibling, mine, nz, terms, layers)
    half, parts[0] = lax.optimization_barrier((half, parts[0]))
    weights = mix(where, mine, other, other, nz, terms, layers, (half,))

    def halves(parts, own):
        held, mid, halo = sort(where, [parts[t] for t in range(QUADS)], own)
        halo = send(
            halo,
            lambda z, q, k: (z + 2 * k - 1, q, 1 - k) if 0 <= z + 2 * k - 1 < layers else None,
        )
        return held, to_core(mid), halo

    held, mid, halo = halves(parts[0], own[0])
    ahead = list(ORDER) if pieces > 1 else []
    for t in ahead[:1]:
        held, parts[1][t] = lax.optimization_barrier((held, parts[1][t]))
    inner = beside = beyond = None
    for piece in range(pieces):
        last = piece == pieces - 1
        inner = ladder("inner", where, held, [], weights, nz, inner)
        mid, inner = lax.optimization_barrier((mid, inner))
        for t in ahead[1:2] if piece == 0 else []:
            mid, parts[1][t] = lax.optimization_barrier((mid, parts[1][t]))
        beside = ladder("beside", where, held, [mid], weights, nz, beside)
        halo, beside = lax.optimization_barrier((halo, beside))
        now, outside = held, halo
        if not last:
            beside, after = lax.optimization_barrier((beside, parts[piece + 1]))
            held, mid, halo = halves(after, own[piece + 1])
            held, outside = lax.optimization_barrier((held, outside))
        beyond = ladder(
            "beyond", where, now, [outside], weights, nz, beyond, (inner, beside) if last else ()
        )
        if not last:
            held, beyond = lax.optimization_barrier((held, beyond))

    stays = (quad >> 1) == core
    pair = jnp.where(stays, beyond[0].astype(jnp.float32), 0.0)
    for v in range(2):
        came = send(beyond[v], lambda z, q, k: (z, 2 * k + (v ^ (q & 1)), q >> 1))
        pair = pair + came.astype(jnp.float32)
    keep = jnp.where(core == 0, pair[0], pair[1])
    give = jnp.where(core == 0, pair[1], pair[0])
    total = keep + to_core(give)
    return lax.psum_scatter(total, "fit", scatter_dimension=1, tiled=True).astype(jnp.bfloat16)


def solution(mesh):
    return jax.shard_map(
        body,
        mesh=mesh,
        in_specs=(
            P("tile", "fit", None, None),
            P("tile", None, None),
            P("tile", None),
            P("tile", None),
            P("tile", None),
            P("tile", None),
        ),
        out_specs=P("tile", "fit", None),
        check_vma=False,
    )
```
